512 devices in a mesh: dp: 32 (over y_lo, z), tensor: 16 (over x, y_hi, core).
Axes of the slice: x: 4, y: 8 (y_hi: 2, y_lo: 4; y = y_hi * 4 + y_lo), z: 8, core: 2. Of those that a mesh axis runs over, the one named last changes fastest.
Arguments:
- emb_input: bfloat16 [4096, 16384], P('dp', 'tensor'), may hold values from -6 to 6
- cross_grad: bfloat16 [4096, 16384], P('dp', 'tensor'), may hold values from -6 to 6
- cross_weight: bfloat16 [16384, 16384], P('tensor', 'dp'), may hold values from -0.046875 to 0.046875
- direct_grad: bfloat16 [4096, 16384], P('tensor', 'dp'), may hold values from -6 to 6
- bag_ids: int32 [4096, 128, 8], P('tensor', 'dp'), may hold values from 0 to 4095
- unit_slots: int32 [32, 16], P('dp'), may hold values from 0 to 15, each once within a row
- table_rows: float32 [32, 16, 1024, 128], P('dp', 'tensor'), may hold values from -6 to 6
- adagrad_acc: float32 [32, 16, 1024], P('dp', 'tensor'), may hold values from 0.1 to 10
Outputs:
- pooled_grad: bfloat16 [4096, 16384], P('tensor', 'dp')
- new_rows: float32 [32, 16, 1024, 128], P('dp', 'tensor')
- new_acc: float32 [32, 16, 1024], P('dp', 'tensor')
The draws below stay inside these ranges and needn't reach their ends.
Inputs may be any that keep to these rules, and one draw needn't show every extreme that they name: Each row of unit_slots names every block number once.
All inputs are finite; a program needn't handle non-finite values.
Results may differ from the reference program's by a relative error of at most 0.019.
Values may be sent and summed in bfloat16 or wider, within the bound.
A program may use at most 64 MiB of HBM per device.

```python
import math
import jax
import jax.numpy as jnp
from jax import lax

TABLES = 128
E = 128
BAG = 8
VB = 1024
D = 16384
BATCH = 4096
TPD = 4
BLOCKS = 4
UNITS = 16
VOCAB = 4096
N_DP = 32
N_TENSOR = 16


def set_ends(result, stream_key, smallest, high):
    shape = result.shape
    spot = [jax.random.randint(jax.random.fold_in(stream_key, axis), (), 0, shape[axis]) for axis in range(len(shape))]
    result = result.at[tuple(spot)].set(smallest)
    longest = shape.index(max(shape))
    spot[longest] = (spot[longest] + 1) % shape[longest]
    return result.at[tuple(spot)].set(high)


def block_scale(stream_key, shape, shards, smallest, largest):
    level, own = 1.0, jax.random.fold_in(stream_key, 6)
    for position, shards_of in shards:
        heights = jnp.exp(jax.random.uniform(jax.random.fold_in(own, position), (shards_of,), jnp.float32, smallest / len(shards), largest / len(shards)))
        level = level * jnp.repeat(heights, shape[position] // shards_of).reshape([-1 if axis == position else 1 for axis in range(len(shape))])
    return level


def normal_values(rng, shape, deviation, bound, split=(), kind=jnp.bfloat16):
    drawn = deviation * jax.random.normal(rng, shape, jnp.float32)
    if split:
        drawn = drawn * block_scale(rng, shape, split, -0.22, 0.18)
    return jnp.clip(drawn, -bound, bound).astype(kind)


def setup_inputs(seed: int = 0) -> dict:
    keys = jax.random.split(jax.random.key(seed), 9)
    return {
        "emb_input": normal_values(keys[0], (BATCH, D), 1.0, 6.0, ((0, 32), (1, 16))),
        "cross_grad": normal_values(keys[1], (BATCH, D), 1.0, 6.0, ((0, 32), (1, 16))),
        "cross_weight": normal_values(keys[2], (D, D), D ** -0.5, 0.046875, ((0, 16), (1, 32))),
        "direct_grad": normal_values(keys[3], (BATCH, D), 1.0, 6.0, ((0, 16), (1, 32))),
        "bag_ids": set_ends(jax.random.randint(keys[4], (BATCH, TABLES, BAG), 0, VOCAB), jax.random.fold_in(keys[4], 1), 0, VOCAB - 1).astype(jnp.int32),
        "unit_slots": jax.vmap(lambda own: jax.random.permutation(own, UNITS))(jax.random.split(keys[5], N_DP)).reshape((N_DP, UNITS)).astype(jnp.int32),
        "table_rows": normal_values(keys[6], (N_DP, UNITS, VB, E), 1.0, 6.0, ((0, 32), (1, 16)), jnp.float32),
        "adagrad_acc": jnp.clip(jnp.exp(math.log(10.0) - 4.6051702 * jax.random.uniform(keys[7], (N_DP, UNITS, VB), jnp.float32) ** block_scale(keys[7], (N_DP, UNITS, VB), ((0, 32), (1, 16)), -0.2, 0.2)), 0.1, 10.0),
    }


learn_rate = 0.5

def reference(emb_input, cross_grad, cross_weight, direct_grad, bag_ids, unit_slots, table_rows, adagrad_acc):
    product = (emb_input.astype(jnp.float32) * cross_grad.astype(jnp.float32)).astype(jnp.bfloat16)
    block_width = D // N_TENSOR

    def add_block(summed_total, block_index):
        row_start = (block_index * block_width).astype(jnp.int32)
        column_piece = lax.dynamic_slice_in_dim(product, row_start, block_width, 1)
        weight_piece = lax.dynamic_slice_in_dim(cross_weight, row_start, block_width, 0)
        partial_value = jnp.dot(column_piece, weight_piece, preferred_element_type=jnp.float32)
        partial_value = lax.optimization_barrier(partial_value.astype(jnp.bfloat16)).astype(jnp.float32)
        return (summed_total + partial_value, None)
    summed_total, _ = lax.scan(add_block, jnp.zeros((BATCH, D), jnp.float32), jnp.arange(N_TENSOR, dtype=jnp.int32))
    pooled_grad = (direct_grad.astype(jnp.float32) + summed_total).astype(jnp.bfloat16)
    pooled_three = pooled_grad.astype(jnp.float32).reshape(BATCH, TABLES, E)

    def table_grad(table_index):
        bag_rows = lax.dynamic_index_in_dim(bag_ids, table_index, 1, keepdims=False)
        grad_rows = lax.dynamic_index_in_dim(pooled_three, table_index, 1, keepdims=False)
        spread = jnp.broadcast_to(grad_rows[:, None, :], (BATCH, BAG, E)).reshape(BATCH * BAG, E)
        return jax.ops.segment_sum(spread, bag_rows.reshape(BATCH * BAG), num_segments=VOCAB)
    all_grads = lax.map(table_grad, jnp.arange(TABLES, dtype=jnp.int32))
    blocked = all_grads.reshape(TABLES, BLOCKS, VB, E)
    dp_position = jnp.arange(N_DP, dtype=jnp.int32)[:, None]
    table_of = dp_position * TPD + unit_slots // BLOCKS
    block_of = unit_slots % BLOCKS
    row_grad = blocked[table_of, block_of]
    new_acc = adagrad_acc + lax.optimization_barrier(jnp.mean(row_grad * row_grad, axis=-1))
    new_rows = table_rows - learn_rate * row_grad / jnp.sqrt(new_acc)[..., None]
    return (pooled_grad, new_rows, new_acc)
```

```python
import jax
import jax.numpy as jnp
from jax import lax
from jax.experimental import pallas as pl
from jax.experimental.pallas import tpu as pltpu
from jax.sharding import PartitionSpec as P

learn_rate = 0.5
F32 = jnp.float32
BF16 = jnp.bfloat16


def kernel(
    emb_ref, cross_ref, weight_ref, direct_ref, ids_ref, slots_ref, rows_ref, acc_ref,
    pooled_ref, new_rows_ref, new_acc_ref,
    factors, blocks, weights, direct, rows, acc_in, acc_wide,
    partial, core_in, summed, from_far, from_minus, from_plus, reduced,
    held, stage, table_grads, ids_stage, ids_all, counts, row_grad, acc_out,
    local_sem, up_send, up_recv, down_send, down_recv, pair_send, pair_recv,
    core_send, core_recv, x_send, far_recv, minus_recv, plus_recv, own_recv,
    final_send, final_recv, half_send, half_recv, table_send, table_recv, ids_send, ids_recv,
):
    dp = lax.axis_index("dp")
    me = lax.axis_index("tensor")
    y, z = dp // 8, dp % 8
    x, h, c = me // 4, (me // 2) % 2, me % 2
    y1 = y + 1 - 2 * (y % 2)
    y2 = (y + 2) % 4
    active = x % 2 == y % 2
    odd = z % 2

    def tensor_of(xx, hh, cc):
        return (xx * 2 + hh) * 2 + cc

    def remote(src, dst, send, recv, to_dp, to_tensor):
        return pltpu.make_async_remote_copy(
            src_ref=src, dst_ref=dst, send_sem=send, recv_sem=recv,
            device_id=(to_dp, to_tensor), device_id_type=pl.DeviceIdType.MESH,
        )

    def arrived(dst, recv, send):
        remote(dst, dst, send, recv, dp, (me + 1) % 16).wait_recv()

    def sent(src, send, recv):
        remote(src, src, send, recv, dp, (me + 1) % 16).wait_send()

    def at_dp(yy, zz):
        return yy * 8 + zz

    barrier = pltpu.get_barrier_semaphore()

    def greet(to_dp, to_tensor):
        pl.semaphore_signal(
            barrier, inc=1, device_id=(to_dp, to_tensor), device_id_type=pl.DeviceIdType.MESH
        )

    up, down = (z + 1) % 8, (z + 7) % 8
    greet(at_dp(y, up), me)
    greet(at_dp(y, down), me)
    greet(at_dp(y2, z), me)
    greet(at_dp(y1, z), me)
    greet(at_dp(y1, z), tensor_of(x, 1 - h, c))

    @pl.loop(1, 16)
    def _(i):
        greet(dp, (me + i) % 16)

    loads = [
        pltpu.make_async_copy(emb_ref, factors.at[0], local_sem.at[0]),
        pltpu.make_async_copy(cross_ref, factors.at[1], local_sem.at[1]),
        pltpu.make_async_copy(weight_ref, weights.at[0], local_sem.at[2]),
        pltpu.make_async_copy(acc_ref, acc_in, local_sem.at[3]),
        pltpu.make_async_copy(direct_ref, direct, local_sem.at[4]),
        pltpu.make_async_copy(rows_ref, rows, local_sem.at[5]),
    ]
    for load in loads:
        load.start()
    loads[0].wait()
    loads[1].wait()

    def place(origin, slot, first=0, count=128):
        start = pl.multiple_of(slot * 256 + (origin % 2) * 128 + first, 64)
        return blocks.at[origin // 2, pl.ds(start, count), :]

    own = place(z, 0)
    own[...] = (factors[0].astype(F32) * factors[1].astype(F32)).astype(BF16)

    pl.semaphore_wait(barrier, 20)

    def ring_up(step, slot):
        origin = (z + 9 - step) % 8
        ref = place(origin, slot, 0, 64 if step == 4 else 128)
        return remote(
            ref, ref, up_send.at[step - 1, slot], up_recv.at[step - 1, slot], at_dp(y, up), me
        )

    def ring_down(step, slot):
        origin = (z + step - 1) % 8
        ref = place(origin, slot, 64, 64) if step == 4 else place(origin, slot)
        return remote(
            ref, ref, down_send.at[step - 1, slot], down_recv.at[step - 1, slot], at_dp(y, down), me
        )

    def ring_start(step, slot):
        ring_up(step, slot).start()
        ring_down(step, slot).start()

    def ring_wait(step, slot):
        low = place((z + 8 - step) % 8, slot, 0, 64 if step == 4 else 128)
        arrived(low, up_recv.at[step - 1, slot], up_send.at[step - 1, slot])
        high_origin = (z + step) % 8
        high = place(high_origin, slot, 64, 64) if step == 4 else place(high_origin, slot)
        arrived(high, down_recv.at[step - 1, slot], down_send.at[step - 1, slot])

    ring_start(1, 0)
    to_pair = remote(
        own, place(z, 1), pair_send.at[0], pair_recv.at[0], at_dp(y2, z), me
    )
    to_pair.start()
    to_side = remote(
        weight_ref, weights.at[1], pair_send.at[1], pair_recv.at[1], at_dp(y1, z), me
    )
    to_side.start()

    def ids_copy(i):
        to = (me + i) % 16
        return remote(
            ids_stage.at[i], ids_all.at[me], ids_send.at[i], ids_recv.at[me], dp, to
        )

    def ids_of(owner):
        table = slots_ref[0, owner]
        value = ids_ref[0]
        for number in range(1, 4):
            value = jnp.where(table == number, ids_ref[number], value)
        return value

    ids_all[me] = ids_of(me)

    @pl.loop(1, 16)
    def _(i):
        ids_stage[i] = ids_of((me + i) % 16)
        ids_copy(i).start()

    loads[3].wait()
    acc_wide[...] = jnp.broadcast_to(acc_in[...], (128, 1024)).T

    first_row = slots_ref[1, me]

    def count(low, high):
        @pl.loop(low, high)
        def _(i):
            source = (me + i) % 16

            @pl.when(i != 0)
            def _():
                arrived(ids_all.at[source], ids_recv.at[source], ids_send.at[i])

            ids = ids_all[source]

            @pl.loop(0, 16)
            def _(r):
                base = pl.multiple_of(r * 64, 64)
                positions = lax.broadcasted_iota(jnp.int32, (64, 256), 0) + (base + first_row)
                total = jnp.zeros((64, 256), F32)
                for bag in range(8):
                    total = total + jnp.where(positions == ids[bag : bag + 1, :], 1.0, 0.0)
                counts[source, pl.ds(base, 64), :] = total.astype(BF16)

    m0 = z // 2
    pair_of = [m0, (m0 + 3 + 2 * odd) % 4, (m0 + 5 - 2 * odd) % 4, (m0 + 2) % 4]
    apart = (2 * h + c - m0 + 4) % 4
    my_step = jnp.where(
        apart == 0, 0, jnp.where(apart == 2, 3, jnp.where(apart == 1, 2 - odd, 1 + odd))
    )

    dest_x = (y + 2 * c) % 4
    ahead = (dest_x - x + 4) % 4

    def multiply(step, side):
        unit = 2 * step + side
        block = pair_of[step]

        @pl.loop(0, 2)
        def _(n):
            cols = pl.ds(pl.multiple_of(n * 256, 256), 256)
            part = jnp.dot(
                blocks[block], weights[side, :, cols], preferred_element_type=F32
            ).astype(BF16)
            partial[unit, 0, :, cols] = part[:256]
            partial[unit, 1, :, cols] = part[256:]

        remote(
            partial.at[unit, 1 - c], core_in.at[unit], core_send.at[unit], core_recv.at[unit],
            dp, tensor_of(x, h, 1 - c),
        ).start()

    def by_rows(body):
        @pl.loop(0, 4)
        def _(r):
            body(pl.ds(pl.multiple_of(r * 64, 64), 64))

    def send_on(step, side):
        unit = 2 * step + side
        to = tensor_of(dest_x, h, pair_of[step] % 2)

        @pl.when(ahead == 1)
        def _():
            remote(
                summed.at[0, unit], from_minus.at[unit], x_send.at[unit], minus_recv.at[unit], dp, to
            ).start()

        @pl.when(ahead == 3)
        def _():
            remote(
                summed.at[0, unit], from_plus.at[unit], x_send.at[unit], plus_recv.at[unit], dp, to
            ).start()

    def combine(step, side):
        unit = 2 * step + side
        arrived(core_in.at[unit], core_recv.at[unit], core_send.at[unit])

        def body(part):
            summed[0, unit, part, :] = (
                partial[unit, c, part, :].astype(F32) + core_in[unit, part, :].astype(F32)
            ).astype(BF16)

        by_rows(body)

        @pl.when((ahead == 0) & (c != pair_of[step] % 2))
        def _():
            remote(
                summed.at[0, unit], summed.at[1, unit], x_send.at[unit], own_recv.at[unit],
                dp, tensor_of(x, h, 1 - c),
            ).start()

        @pl.when(ahead == 2)
        def _():
            relay = (x + (1 if side == 0 else 3)) % 4
            remote(
                summed.at[0, unit], from_far.at[unit], x_send.at[unit], far_recv.at[unit],
                dp, tensor_of(relay, h, c),
            ).start()

        @pl.when(ahead == (3 if side == 0 else 1))
        def _():
            send_on(step, side)

    def relay_on(step, side):
        unit = 2 * step + side

        @pl.when(ahead == (1 if side == 0 else 3))
        def _():
            arrived(from_far.at[unit], far_recv.at[unit], x_send.at[unit])

            def body(part):
                summed[0, unit, part, :] = (
                    summed[0, unit, part, :].astype(F32) + from_far[unit, part, :].astype(F32)
                ).astype(BF16)

            by_rows(body)
            send_on(step, side)

    other_core = jnp.where((x == y) == (c == 0), 0, 1)

    def reduces(step):
        return active & (c == pair_of[step] % 2)

    def final_remote(step, side):
        unit = 2 * step + side
        home = pair_of[step] // 2
        here = 1 - (home - h) * (home - h)
        return remote(
            reduced.at[unit], reduced.at[9 - here], final_send.at[unit], final_recv.at[1 - here],
            at_dp(y1 if side else y, z), tensor_of(x, home, c),
        )

    def stays(step, side):
        return (pair_of[step] // 2 == h) if side == 0 else False

    def reduce_x(step, side):
        unit = 2 * step + side

        @pl.when(reduces(step))
        def _():
            @pl.when(other_core == 1)
            def _():
                arrived(summed.at[1, unit], own_recv.at[unit], x_send.at[unit])

            arrived(from_minus.at[unit], minus_recv.at[unit], x_send.at[unit])
            arrived(from_plus.at[unit], plus_recv.at[unit], x_send.at[unit])
            if side == 0:
                home = pair_of[step] // 2
                target = jnp.where(home == h, 8, unit)
            else:
                target = unit

            def body(part):
                reduced[target, part, :] = (
                    summed[other_core, unit, part, :].astype(F32)
                    + from_minus[unit, part, :].astype(F32)
                    + from_plus[unit, part, :].astype(F32)
                ).astype(BF16)

            by_rows(body)
            if side == 0:

                @pl.when(pair_of[step] // 2 != h)
                def _():
                    final_remote(step, side).start()

            else:
                final_remote(step, side).start()

    def table_copy(half, i):
        spot = ((2 * x + c) + i) % 8
        to = tensor_of(spot // 2, h, spot % 2)
        source = tensor_of(x, (h + half) % 2, c)
        return remote(
            stage.at[half, i], table_grads.at[source], table_send.at[half, i],
            table_recv.at[source], dp, to,
        )

    def send_tables(half):
        source = tensor_of(x, (h + half) % 2, c)

        def chosen(owner):
            table = slots_ref[0, owner]
            value = held[half, :, 0:128]
            for number in range(1, 4):
                columns = held[half, :, 128 * number : 128 * (number + 1)]
                value = jnp.where(table == number, columns, value)
            return value

        @pl.loop(1, 8)
        def _(i):
            spot = ((2 * x + c) + i) % 8
            stage[half, i] = chosen(tensor_of(spot // 2, h, spot % 2))
            table_copy(half, i).start()

        table_grads[source] = chosen(me)

    to_half = remote(
        held.at[0], held.at[1], half_send.at[0], half_recv.at[0], dp, tensor_of(x, 1 - h, c)
    )
    write_pooled = pltpu.make_async_copy(held.at[0], pooled_ref, local_sem.at[6])

    def finish_pooled():
        @pl.when(jnp.logical_not(active))
        def _():
            arrived(reduced.at[8], final_recv.at[0], final_send.at[0])

        arrived(reduced.at[9], final_recv.at[1], final_send.at[0])

        def body(part):
            held[0, part, :] = (
                direct[part, :].astype(F32)
                + (reduced[8, part, :].astype(F32) + reduced[9, part, :].astype(F32))
            ).astype(BF16)

        by_rows(body)
        to_half.start()
        write_pooled.start()
        send_tables(0)

    def finish_other():
        arrived(held.at[1], half_recv.at[0], half_send.at[0])
        send_tables(1)

    def scatter(step):
        @pl.loop(0, 4)
        def _(xx):
            source = 4 * xx + pair_of[step]

            @pl.when((xx != x) | (pair_of[step] % 2 != c))
            def _():
                arrived(table_grads.at[source], table_recv.at[source], table_send.at[0, 1])

            row_grad[...] += jnp.dot(
                counts[source], table_grads[source], preferred_element_type=F32
            )

    row_grad[...] = jnp.zeros_like(row_grad)
    arrived(place(z, 1), pair_recv.at[0], pair_send.at[0])
    ring_start(1, 1)
    loads[2].wait()
    ring_wait(1, 0)
    ring_start(2, 0)
    count(0, 3)
    ring_wait(1, 1)
    ring_start(2, 1)
    multiply(0, 0)
    count(3, 6)
    ring_wait(2, 0)
    ring_start(3, 0)
    combine(0, 0)
    count(6, 9)
    ring_wait(2, 1)
    ring_start(3, 1)
    multiply(1, 0)
    relay_on(0, 0)
    count(9, 12)
    combine(1, 0)
    ring_wait(3, 0)
    ring_start(4, 0)
    reduce_x(0, 0)
    relay_on(1, 0)
    count(12, 16)
    loads[4].wait()
    loads[5].wait()
    ring_wait(3, 1)
    ring_start(4, 1)
    arrived(weights.at[1], pair_recv.at[1], pair_send.at[1])
    multiply(0, 1)
    multiply(1, 1)
    combine(0, 1)
    multiply(2, 0)
    combine(1, 1)
    multiply(2, 1)
    relay_on(0, 1)
    relay_on(1, 1)
    combine(2, 0)
    combine(2, 1)
    ring_wait(4, 0)
    ring_wait(4, 1)
    multiply(3, 0)
    multiply(3, 1)
    relay_on(2, 0)
    relay_on(2, 1)
    combine(3, 0)
    combine(3, 1)
    reduce_x(1, 0)
    reduce_x(0, 1)
    reduce_x(1, 1)
    relay_on(3, 0)
    reduce_x(2, 0)
    relay_on(3, 1)
    reduce_x(2, 1)

    @pl.when(my_step != 3)
    def _():
        finish_pooled()

    @pl.when(my_step != 0)
    def _():
        finish_other()

    reduce_x(3, 0)
    reduce_x(3, 1)

    @pl.when(my_step == 3)
    def _():
        finish_pooled()

    @pl.when(my_step == 0)
    def _():
        finish_other()

    scatter(0)
    scatter(1)
    scatter(2)
    scatter(3)

    new_acc = acc_wide[...] + jnp.mean(row_grad[...] * row_grad[...], axis=-1, keepdims=True)
    rows[...] = rows[...] - learn_rate * row_grad[...] / jnp.sqrt(new_acc)
    acc_out[...] = new_acc.T[0:1, :]
    write_rows = pltpu.make_async_copy(rows, new_rows_ref, local_sem.at[7])
    write_acc = pltpu.make_async_copy(acc_out, new_acc_ref, local_sem.at[8])
    write_rows.start()
    write_acc.start()

    for step in range(1, 5):
        for slot in range(2):
            ring_up(step, slot).wait_send()
            ring_down(step, slot).wait_send()
    to_pair.wait_send()
    to_side.wait_send()

    @pl.loop(1, 16)
    def _(i):
        ids_copy(i).wait_send()

    for step in range(4):
        for side in range(2):
            unit = 2 * step + side
            sent(partial.at[unit, 0], core_send.at[unit], core_recv.at[unit])

            @pl.when((ahead != 0) | (c != pair_of[step] % 2))
            def _():
                sent(summed.at[0, unit], x_send.at[unit], own_recv.at[unit])

            away = reduces(step)
            if side == 0:
                away = away & (pair_of[step] // 2 != h)

            @pl.when(away)
            def _():
                sent(reduced.at[unit], final_send.at[unit], final_recv.at[0])

    to_half.wait_send()

    @pl.loop(1, 8)
    def _(i):
        table_copy(0, i).wait_send()
        table_copy(1, i).wait_send()

    write_pooled.wait()
    write_rows.wait()
    write_acc.wait()


def local(
    emb_input, cross_grad, cross_weight, direct_grad, bag_ids, unit_slots, table_rows, adagrad_acc
):
    anywhere = pl.BlockSpec(memory_space=pl.ANY)
    dma = pltpu.SemaphoreType.DMA
    pooled, new_rows, new_acc = pl.pallas_call(
        kernel,
        out_shape=(
            jax.ShapeDtypeStruct((256, 512), BF16),
            jax.ShapeDtypeStruct((1024, 128), F32),
            jax.ShapeDtypeStruct((1, 1024), F32),
        ),
        in_specs=[anywhere] * 4
        + [pl.BlockSpec(memory_space=pltpu.VMEM), pl.BlockSpec(memory_space=pltpu.SMEM)]
        + [anywhere] * 2,
        out_specs=(anywhere,) * 3,
        scratch_shapes=[
            pltpu.VMEM((2, 128, 1024), BF16),
            pltpu.VMEM((4, 512, 1024), BF16),
            pltpu.VMEM((2, 1024, 512), BF16),
            pltpu.VMEM((256, 512), BF16),
            pltpu.VMEM((1024, 128), F32),
            pltpu.VMEM((1, 1024), F32),
            pltpu.VMEM((1024, 128), F32),
            pltpu.VMEM((8, 2, 256, 512), BF16),
            pltpu.VMEM((8, 256, 512), BF16),
            pltpu.VMEM((2, 8, 256, 512), BF16),
            pltpu.VMEM((8, 256, 512), BF16),
            pltpu.VMEM((8, 256, 512), BF16),
            pltpu.VMEM((8, 256, 512), BF16),
            pltpu.VMEM((10, 256, 512), BF16),
            pltpu.VMEM((2, 256, 512), BF16),
            pltpu.VMEM((2, 8, 256, 128), BF16),
            pltpu.VMEM((16, 256, 128), BF16),
            pltpu.VMEM((16, 8, 256), jnp.int32),
            pltpu.VMEM((16, 8, 256), jnp.int32),
            pltpu.VMEM((16, 1024, 256), BF16),
            pltpu.VMEM((1024, 128), F32),
            pltpu.VMEM((1, 1024), F32),
            dma((9,)),
            dma((4, 2)),
            dma((4, 2)),
            dma((4, 2)),
            dma((4, 2)),
            dma((2,)),
            dma((2,)),
            dma((8,)),
            dma((8,)),
            dma((8,)),
            dma((8,)),
            dma((8,)),
            dma((8,)),
            dma((8,)),
            dma((8,)),
            dma((2,)),
            dma((1,)),
            dma((1,)),
            dma((2, 8)),
            dma((16,)),
            dma((16,)),
            dma((16,)),
        ],
        compiler_params=pltpu.CompilerParams(
            collective_id=1, has_side_effects=True, vmem_limit_bytes=56 * 2**20
        ),
        cost_estimate=pl.CostEstimate(
            flops=5_400_000_000, bytes_accessed=4_000_000, transcendentals=1024
        ),
    )(
        emb_input,
        cross_grad,
        cross_weight,
        direct_grad,
        jnp.transpose(bag_ids, (1, 2, 0)),
        jnp.concatenate([unit_slots // 4, unit_slots % 4 * 1024]),
        table_rows[0, 0],
        adagrad_acc[0],
    )
    return (pooled, new_rows[None, None], new_acc[None])


def solution(mesh):
    return jax.shard_map(
        local,
        mesh=mesh,
        in_specs=(
            P("dp", "tensor"),
            P("dp", "tensor"),
            P("tensor", "dp"),
            P("tensor", "dp"),
            P("tensor", "dp", None),
            P("dp", None),
            P("dp", "tensor", None, None),
            P("dp", "tensor", None),
        ),
        out_specs=(P("tensor", "dp"), P("dp", "tensor", None, None), P("dp", "tensor", None)),
        check_vma=False,
    )
```

```python
import jax
import jax.numpy as jnp
from jax import lax
from jax.experimental import pallas as pl
from jax.experimental.pallas import tpu as pltpu
from jax.sharding import PartitionSpec as P

learn_rate = 0.5
F32 = jnp.float32
BF16 = jnp.bfloat16


def kernel(
    emb_ref, cross_ref, weight_ref, direct_ref, ids_ref, slots_ref,
    pooled_ref, row_grad_ref,
    factors, blocks, weights, direct,
    partial, core_in, summed, from_far, from_minus, from_plus, reduced,
    held, stage, table_grads, ids_stage, ids_all, packed, counts, row_grad,
    local_sem, up_send, up_recv, down_send, down_recv, pair_send, pair_recv,
    core_send, core_recv, x_send, far_recv, minus_recv, plus_recv, own_recv,
    final_send, final_recv, table_send, table_recv, ids_send, ids_recv,
):
    dp = lax.axis_index("dp")
    me = lax.axis_index("tensor")
    y, z = dp // 8, dp % 8
    x, h, c = me // 4, (me // 2) % 2, me % 2
    y1 = y + 1 - 2 * (y % 2)
    y2 = (y + 2) % 4
    active = x % 2 == y % 2
    odd = z % 2

    def tensor_of(xx, hh, cc):
        return (xx * 2 + hh) * 2 + cc

    def remote(src, dst, send, recv, to_dp, to_tensor):
        return pltpu.make_async_remote_copy(
            src_ref=src, dst_ref=dst, send_sem=send, recv_sem=recv,
            device_id=(to_dp, to_tensor), device_id_type=pl.DeviceIdType.MESH,
        )

    def arrived(dst, recv, send):
        remote(dst, dst, send, recv, dp, (me + 1) % 16).wait_recv()

    def sent(src, send, recv):
        remote(src, src, send, recv, dp, (me + 1) % 16).wait_send()

    def at_dp(yy, zz):
        return yy * 8 + zz

    barrier = pltpu.get_barrier_semaphore()

    def greet(to_dp, to_tensor):
        pl.semaphore_signal(
            barrier, inc=1, device_id=(to_dp, to_tensor), device_id_type=pl.DeviceIdType.MESH
        )

    up, down = (z + 1) % 8, (z + 7) % 8
    greet(at_dp(y, up), me)
    greet(at_dp(y, down), me)
    greet(at_dp(y2, z), me)
    greet(at_dp(y1, z), me)
    greet(at_dp(y1, z), tensor_of(x, 1 - h, c))

    @pl.loop(1, 16)
    def _(i):
        greet(dp, (me + i) % 16)

    loads = [
        pltpu.make_async_copy(emb_ref, factors.at[0], local_sem.at[0]),
        pltpu.make_async_copy(cross_ref, factors.at[1], local_sem.at[1]),
        pltpu.make_async_copy(weight_ref, weights.at[0], local_sem.at[2]),
        pltpu.make_async_copy(direct_ref, direct.at[0], local_sem.at[3]),
    ]
    for load in loads:
        load.start()
    loads[0].wait()
    loads[1].wait()

    def place(origin, slot, first=0, count=128):
        start = pl.multiple_of(slot * 256 + (origin % 2) * 128 + first, 64)
        return blocks.at[origin // 2, pl.ds(start, count), :]

    own = place(z, 0)
    own[...] = (factors[0].astype(F32) * factors[1].astype(F32)).astype(BF16)

    pl.semaphore_wait(barrier, 20)

    def ring_up(step, slot):
        origin = (z + 9 - step) % 8
        ref = place(origin, slot, 0, 64 if step == 4 else 128)
        return remote(
            ref, ref, up_send.at[step - 1, slot], up_recv.at[step - 1, slot], at_dp(y, up), me
        )

    def ring_down(step, slot):
        origin = (z + step - 1) % 8
        ref = place(origin, slot, 64, 64) if step == 4 else place(origin, slot)
        return remote(
            ref, ref, down_send.at[step - 1, slot], down_recv.at[step - 1, slot], at_dp(y, down), me
        )

    def ring_start(step, slot):
        ring_up(step, slot).start()
        ring_down(step, slot).start()

    def ring_wait(step, slot):
        low = place((z + 8 - step) % 8, slot, 0, 64 if step == 4 else 128)
        arrived(low, up_recv.at[step - 1, slot], up_send.at[step - 1, slot])
        high_origin = (z + step) % 8
        high = place(high_origin, slot, 64, 64) if step == 4 else place(high_origin, slot)
        arrived(high, down_recv.at[step - 1, slot], down_send.at[step - 1, slot])

    ring_start(1, 0)
    to_pair = remote(
        own, place(z, 1), pair_send.at[0], pair_recv.at[0], at_dp(y2, z), me
    )
    to_pair.start()
    to_side = remote(
        weight_ref, weights.at[1], pair_send.at[1], pair_recv.at[1], at_dp(y1, z), me
    )

    to_other = remote(
        direct_ref, direct.at[1], pair_send.at[2], pair_recv.at[2], dp, tensor_of(x, 1 - h, c)
    )

    def ids_copy(i):
        to = (me + i) % 16
        return remote(
            ids_stage.at[i], ids_all.at[me], ids_send.at[i], ids_recv.at[me], dp, to
        )

    def ids_of(owner):
        slot = slots_ref[0, owner]
        value = ids_ref[0]
        for number in range(1, 4):
            value = jnp.where(slot >= 4 * number, ids_ref[number], value)
        return value

    ids_all[me] = ids_of(me)

    @pl.loop(1, 16)
    def _(i):
        ids_stage[i] = ids_of((me + i) % 16)
        ids_copy(i).start()

    first_row = (slots_ref[0, me] & 3) * 1024

    def count(low, high):
        @pl.loop(low, high)
        def _(i):
            source = (me + i) % 16

            @pl.when(i != 0)
            def _():
                arrived(ids_all.at[source], ids_recv.at[source], ids_send.at[i])

            ids = ids_all[source] - first_row
            digit = jnp.where((ids & 1) != 0, 16, 1) * jnp.where((ids & 2) != 0, 256, 1)
            digit = digit * jnp.where((ids & 4) != 0, 65536, 1)
            word = lax.shift_right_arithmetic(ids, 3)
            numbers = lax.broadcasted_iota(jnp.int32, (128, 256), 0)
            total = jnp.zeros((128, 256), jnp.int32)
            for bag in range(8):
                total = total + jnp.where(
                    numbers == word[bag : bag + 1, :], digit[bag : bag + 1, :], 0
                )
            packed[...] = total
            shifts = 4 * lax.broadcasted_iota(jnp.int32, (8, 256), 0)
            cols = pl.ds(pl.multiple_of((source // 4) * 256, 256), 256)

            @pl.loop(0, 8)
            def _(r):
                words = packed[pl.ds(pl.multiple_of(r * 16, 16), 16), :]
                for n in range(8):
                    both = [
                        lax.shift_right_logical(
                            jnp.broadcast_to(words[k : k + 1, :], (8, 256)), shifts
                        )
                        & 15
                        for k in (2 * n, 2 * n + 1)
                    ]
                    counts[
                        source % 4, pl.ds(pl.multiple_of(r * 128 + n * 16, 16), 16), cols
                    ] = jnp.concatenate(both).astype(F32).astype(BF16)

    m0 = z // 2
    pair_of = [m0, (m0 + 3 + 2 * odd) % 4, (m0 + 5 - 2 * odd) % 4, (m0 + 2) % 4]
    dest_x = (y + 2 * c) % 4
    ahead = (dest_x - x + 4) % 4

    def multiply(step, side):
        unit = 2 * step + side
        block = pair_of[step]

        @pl.loop(0, 2)
        def _(n):
            cols = pl.ds(pl.multiple_of(n * 256, 256), 256)
            part = jnp.dot(
                blocks[block], weights[side, :, cols], preferred_element_type=F32
            ).astype(BF16)
            partial[unit, 0, :, cols] = part[:256]
            partial[unit, 1, :, cols] = part[256:]

        remote(
            partial.at[unit, 1 - c], core_in.at[unit], core_send.at[unit], core_recv.at[unit],
            dp, tensor_of(x, h, 1 - c),
        ).start()

    def by_rows(body):
        @pl.loop(0, 4)
        def _(r):
            body(pl.ds(pl.multiple_of(r * 64, 64), 64))

    def send_on(step, side):
        unit = 2 * step + side
        to = tensor_of(dest_x, h, pair_of[step] % 2)

        @pl.when(ahead == 1)
        def _():
            remote(
                summed.at[0, unit], from_minus.at[unit], x_send.at[unit], minus_recv.at[unit], dp, to
            ).start()

        @pl.when(ahead == 3)
        def _():
            remote(
                summed.at[0, unit], from_plus.at[unit], x_send.at[unit], plus_recv.at[unit], dp, to
            ).start()

    def combine(step, side):
        unit = 2 * step + side
        arrived(core_in.at[unit], core_recv.at[unit], core_send.at[unit])

        def body(part):
            summed[0, unit, part, :] = (
                partial[unit, c, part, :].astype(F32) + core_in[unit, part, :].astype(F32)
            ).astype(BF16)

        by_rows(body)

        @pl.when((ahead == 0) & (c != pair_of[step] % 2))
        def _():
            remote(
                summed.at[0, unit], summed.at[1, unit], x_send.at[unit], own_recv.at[unit],
                dp, tensor_of(x, h, 1 - c),
            ).start()

        @pl.when(ahead == 2)
        def _():
            relay = (x + (1 if side == 0 else 3)) % 4
            remote(
                summed.at[0, unit], from_far.at[unit], x_send.at[unit], far_recv.at[unit],
                dp, tensor_of(relay, h, c),
            ).start()

        @pl.when(ahead == (3 if side == 0 else 1))
        def _():
            send_on(step, side)

    def relay_on(step, side):
        unit = 2 * step + side

        @pl.when(ahead == (1 if side == 0 else 3))
        def _():
            arrived(from_far.at[unit], far_recv.at[unit], x_send.at[unit])

            def body(part):
                summed[0, unit, part, :] = (
                    summed[0, unit, part, :].astype(F32) + from_far[unit, part, :].astype(F32)
                ).astype(BF16)

            by_rows(body)
            send_on(step, side)

    other_core = jnp.where((x == y) == (c == 0), 0, 1)

    def reduces(step):
        return active & (c == pair_of[step] % 2)

    def half_of(step):
        home = pair_of[step] // 2
        return (home - h) * (home - h)

    def final_remotes(step, side):
        unit = 2 * step + side
        half = half_of(step)
        same, across = 8 + 2 * half, 11 - 2 * half
        source = reduced.at[unit if side else same]
        copies = [
            remote(
                source, reduced.at[across], final_send.at[unit, 0], final_recv.at[across - 8],
                at_dp(y1 if side else y, z), tensor_of(x, 1 - h, c),
            )
        ]
        if side:
            copies.append(
                remote(
                    source, reduced.at[same], final_send.at[unit, 1], final_recv.at[same - 8],
                    at_dp(y1, z), me,
                )
            )
        return copies

    def reduce_x(step, side):
        unit = 2 * step + side

        @pl.when(reduces(step))
        def _():
            @pl.when(other_core == 1)
            def _():
                arrived(summed.at[1, unit], own_recv.at[unit], x_send.at[unit])

            arrived(from_minus.at[unit], minus_recv.at[unit], x_send.at[unit])
            arrived(from_plus.at[unit], plus_recv.at[unit], x_send.at[unit])
            target = unit if side else 8 + 2 * half_of(step)

            def body(part):
                reduced[target, part, :] = (
                    summed[other_core, unit, part, :].astype(F32)
                    + from_minus[unit, part, :].astype(F32)
                    + from_plus[unit, part, :].astype(F32)
                ).astype(BF16)

            by_rows(body)
            for copy in final_remotes(step, side):
                copy.start()

    def table_copy(half, i):
        spot = ((2 * x + c) + i) % 8
        to = tensor_of(spot // 2, h, spot % 2)
        source = tensor_of(x, (h + half) % 2, c)
        return remote(
            stage.at[half, i], table_grads.at[source % 4, source // 4], table_send.at[half, i],
            table_recv.at[source], dp, to,
        )

    def send_tables(half):
        source = tensor_of(x, (h + half) % 2, c)

        def chosen(owner):
            slot = slots_ref[0, owner]
            value = held[half, :, 0:128]
            for number in range(1, 4):
                columns = held[half, :, 128 * number : 128 * (number + 1)]
                value = jnp.where(slot >= 4 * number, columns, value)
            return value

        @pl.loop(1, 8)
        def _(i):
            spot = ((2 * x + c) + i) % 8
            stage[half, i] = chosen(tensor_of(spot // 2, h, spot % 2))
            table_copy(half, i).start()

        table_grads[source % 4, source // 4] = chosen(me)

    write_pooled = pltpu.make_async_copy(held.at[0], pooled_ref, local_sem.at[4])

    def finish(half):
        here, across = 8 + 2 * half, 9 + 2 * half

        @pl.when(jnp.logical_not(active))
        def _():
            arrived(reduced.at[here], final_recv.at[here - 8], final_send.at[0, 0])

        arrived(reduced.at[across], final_recv.at[across - 8], final_send.at[0, 0])

        def body(part):
            held[half, part, :] = (
                direct[half, part, :].astype(F32)
                + (reduced[here, part, :].astype(F32) + reduced[across, part, :].astype(F32))
            ).astype(BF16)

        by_rows(body)
        if half == 0:
            write_pooled.start()
        send_tables(half)

    def finish_step(step):
        @pl.when(c == pair_of[step] % 2)
        def _():
            @pl.when(half_of(step) == 0)
            def _():
                finish(0)

            @pl.when(half_of(step) == 1)
            def _():
                finish(1)

    def scatter(step):
        block = pair_of[step]

        @pl.loop(0, 4)
        def _(xx):
            source = 4 * xx + block

            @pl.when((xx != x) | (block % 2 != c))
            def _():
                arrived(table_grads.at[block, xx], table_recv.at[source], table_send.at[0, 1])

        part = jnp.dot(
            counts[block],
            table_grads[block].reshape(1024, 128),
            preferred_element_type=F32,
        )
        if step == 0:
            row_grad[...] = part
        else:
            row_grad[...] += part

    ring_wait(1, 0)
    ring_start(2, 0)
    count(0, 4)
    arrived(place(z, 1), pair_recv.at[0], pair_send.at[0])
    ring_start(1, 1)
    to_side.start()
    ring_wait(2, 0)
    ring_start(3, 0)
    count(4, 12)
    ring_wait(1, 1)
    ring_start(2, 1)
    loads[2].wait()
    multiply(0, 0)
    count(12, 16)
    ring_wait(3, 0)
    ring_start(4, 0)
    combine(0, 0)
    loads[3].wait()
    ring_wait(2, 1)
    ring_start(3, 1)
    multiply(1, 0)
    relay_on(0, 0)
    combine(1, 0)
    arrived(weights.at[1], pair_recv.at[1], pair_send.at[1])
    to_other.start()
    multiply(0, 1)
    multiply(1, 1)
    reduce_x(0, 0)
    combine(0, 1)
    combine(1, 1)
    relay_on(1, 0)
    ring_wait(3, 1)
    ring_start(4, 1)
    multiply(2, 0)
    multiply(2, 1)
    relay_on(0, 1)
    combine(2, 0)
    relay_on(1, 1)
    combine(2, 1)
    reduce_x(1, 0)
    reduce_x(0, 1)
    relay_on(2, 0)
    ring_wait(4, 0)
    ring_wait(4, 1)
    multiply(3, 0)
    multiply(3, 1)
    relay_on(2, 1)
    combine(3, 0)
    combine(3, 1)
    reduce_x(1, 1)

    relay_on(3, 0)
    reduce_x(2, 0)
    relay_on(3, 1)
    reduce_x(2, 1)

    reduce_x(3, 0)
    reduce_x(3, 1)
    arrived(direct.at[1], pair_recv.at[2], pair_send.at[2])
    finish_step(0)
    finish_step(1)
    finish_step(2)
    finish_step(3)
    scatter(0)
    scatter(1)
    scatter(2)
    scatter(3)
    write_rows = pltpu.make_async_copy(row_grad, row_grad_ref, local_sem.at[5])
    write_rows.start()

    for step in range(1, 5):
        for slot in range(2):
            ring_up(step, slot).wait_send()
            ring_down(step, slot).wait_send()
    to_pair.wait_send()
    to_side.wait_send()
    to_other.wait_send()

    @pl.loop(1, 16)
    def _(i):
        ids_copy(i).wait_send()

    for step in range(4):
        for side in range(2):
            unit = 2 * step + side
            sent(partial.at[unit, 0], core_send.at[unit], core_recv.at[unit])

            @pl.when((ahead != 0) | (c != pair_of[step] % 2))
            def _():
                sent(summed.at[0, unit], x_send.at[unit], own_recv.at[unit])

            @pl.when(reduces(step))
            def _():
                for copy in final_remotes(step, side):
                    copy.wait_send()

    @pl.loop(1, 8)
    def _(i):
        table_copy(0, i).wait_send()
        table_copy(1, i).wait_send()

    write_pooled.wait()
    write_rows.wait()


def local(
    emb_input, cross_grad, cross_weight, direct_grad, bag_ids, unit_slots, table_rows, adagrad_acc
):
    anywhere = pl.BlockSpec(memory_space=pl.ANY)
    dma = pltpu.SemaphoreType.DMA
    pooled, row_grad = pl.pallas_call(
        kernel,
        out_shape=(
            jax.ShapeDtypeStruct((256, 512), BF16),
            jax.ShapeDtypeStruct((1024, 128), F32),
        ),
        in_specs=[anywhere] * 4
        + [pl.BlockSpec(memory_space=pltpu.VMEM), pl.BlockSpec(memory_space=pltpu.SMEM)],
        out_specs=(anywhere,) * 2,
        scratch_shapes=[
            pltpu.VMEM((2, 128, 1024), BF16),
            pltpu.VMEM((4, 512, 1024), BF16),
            pltpu.VMEM((2, 1024, 512), BF16),
            pltpu.VMEM((2, 256, 512), BF16),
            pltpu.VMEM((8, 2, 256, 512), BF16),
            pltpu.VMEM((8, 256, 512), BF16),
            pltpu.VMEM((2, 8, 256, 512), BF16),
            pltpu.VMEM((8, 256, 512), BF16),
            pltpu.VMEM((8, 256, 512), BF16),
            pltpu.VMEM((8, 256, 512), BF16),
            pltpu.VMEM((12, 256, 512), BF16),
            pltpu.VMEM((2, 256, 512), BF16),
            pltpu.VMEM((2, 8, 256, 128), BF16),
            pltpu.VMEM((4, 4, 256, 128), BF16),
            pltpu.VMEM((16, 8, 256), jnp.int32),
            pltpu.VMEM((16, 8, 256), jnp.int32),
            pltpu.VMEM((128, 256), jnp.int32),
            pltpu.VMEM((4, 1024, 1024), BF16),
            pltpu.VMEM((1024, 128), F32),
            dma((6,)),
            dma((4, 2)),
            dma((4, 2)),
            dma((4, 2)),
            dma((4, 2)),
            dma((3,)),
            dma((3,)),
            dma((8,)),
            dma((8,)),
            dma((8,)),
            dma((8,)),
            dma((8,)),
            dma((8,)),
            dma((8,)),
            dma((8, 2)),
            dma((4,)),
            dma((2, 8)),
            dma((16,)),
            dma((16,)),
            dma((16,)),
        ],
        compiler_params=pltpu.CompilerParams(
            collective_id=1, has_side_effects=True, vmem_limit_bytes=56 * 2**20
        ),
        cost_estimate=pl.CostEstimate(
            flops=5_400_000_000, bytes_accessed=4_000_000, transcendentals=1024
        ),
    )(
        emb_input,
        cross_grad,
        cross_weight,
        direct_grad,
        jnp.transpose(bag_ids, (1, 2, 0)),
        unit_slots,
    )
    new_acc = adagrad_acc[0, 0] + jnp.mean(row_grad * row_grad, axis=-1)
    new_rows = table_rows[0, 0] - learn_rate * row_grad / jnp.sqrt(new_acc)[:, None]
    return (pooled, new_rows[None, None], new_acc[None, None])


def solution(mesh):
    return jax.shard_map(
        local,
        mesh=mesh,
        in_specs=(
            P("dp", "tensor"),
            P("dp", "tensor"),
            P("tensor", "dp"),
            P("tensor", "dp"),
            P("tensor", "dp", None),
            P("dp", None),
            P("dp", "tensor", None, None),
            P("dp", "tensor", None),
        ),
        out_specs=(P("tensor", "dp"), P("dp", "tensor", None, None), P("dp", "tensor", None)),
        check_vma=False,
    )
```

```python
import jax
import jax.numpy as jnp
from jax import lax
from jax.experimental import pallas as pl
from jax.experimental.pallas import tpu as pltpu
from jax.sharding import PartitionSpec as P

learn_rate = 0.5
F32 = jnp.float32
BF16 = jnp.bfloat16


def kernel(
    emb_ref, cross_ref, weight_ref, direct_ref, ids_ref, slots_ref,
    pooled_ref, row_grad_ref,
    factors, blocks, weights, direct,
    partial, core_in, summed, from_far, from_minus, from_plus, reduced,
    held, stage, table_grads, ids_stage, ids_all, packed, counts, row_grad,
    local_sem, up_send, up_recv, down_send, down_recv, pair_send, pair_recv,
    core_send, core_recv, x_send, far_recv, minus_recv, plus_recv, own_recv,
    final_send, final_recv, table_send, table_recv, ids_send, ids_recv,
):
    dp = lax.axis_index("dp")
    me = lax.axis_index("tensor")
    y, z = dp // 8, dp % 8
    x, h, c = me // 4, (me // 2) % 2, me % 2
    y1 = y + 1 - 2 * (y % 2)
    y2 = (y + 2) % 4
    active = x % 2 == y % 2
    odd = z % 2

    def tensor_of(xx, hh, cc):
        return (xx * 2 + hh) * 2 + cc

    def remote(src, dst, send, recv, to_dp, to_tensor):
        return pltpu.make_async_remote_copy(
            src_ref=src, dst_ref=dst, send_sem=send, recv_sem=recv,
            device_id=(to_dp, to_tensor), device_id_type=pl.DeviceIdType.MESH,
        )

    def arrived(dst, recv, send):
        remote(dst, dst, send, recv, dp, (me + 1) % 16).wait_recv()

    def sent(src, send, recv):
        remote(src, src, send, recv, dp, (me + 1) % 16).wait_send()

    def at_dp(yy, zz):
        return yy * 8 + zz

    barrier = pltpu.get_barrier_semaphore()

    def greet(to_dp, to_tensor):
        pl.semaphore_signal(
            barrier, inc=1, device_id=(to_dp, to_tensor), device_id_type=pl.DeviceIdType.MESH
        )

    up, down = (z + 1) % 8, (z + 7) % 8
    greet(at_dp(y, up), me)
    greet(at_dp(y, down), me)
    greet(at_dp(y2, z), me)
    greet(at_dp(y1, z), me)
    greet(at_dp(y1, z), tensor_of(x, 1 - h, c))

    @pl.loop(1, 16)
    def _(i):
        greet(dp, (me + i) % 16)

    loads = [
        pltpu.make_async_copy(emb_ref, factors.at[0], local_sem.at[0]),
        pltpu.make_async_copy(cross_ref, factors.at[1], local_sem.at[1]),
        pltpu.make_async_copy(weight_ref, weights.at[0], local_sem.at[2]),
        pltpu.make_async_copy(direct_ref, direct.at[0], local_sem.at[3]),
    ]
    for load in loads:
        load.start()
    loads[0].wait()
    loads[1].wait()

    def place(origin, slot, first=0, count=128):
        start = pl.multiple_of(slot * 256 + (origin % 2) * 128 + first, 64)
        return blocks.at[origin // 2, pl.ds(start, count), :]

    own = place(z, 0)
    own[...] = (factors[0].astype(F32) * factors[1].astype(F32)).astype(BF16)

    pl.semaphore_wait(barrier, 20)

    def ring_up(step, slot):
        origin = (z + 9 - step) % 8
        ref = place(origin, slot, 0, 64 if step == 4 else 128)
        return remote(
            ref, ref, up_send.at[step - 1, slot], up_recv.at[step - 1, slot], at_dp(y, up), me
        )

    def ring_down(step, slot):
        origin = (z + step - 1) % 8
        ref = place(origin, slot, 64, 64) if step == 4 else place(origin, slot)
        return remote(
            ref, ref, down_send.at[step - 1, slot], down_recv.at[step - 1, slot], at_dp(y, down), me
        )

    def ring_start(step, slot):
        ring_up(step, slot).start()
        ring_down(step, slot).start()

    def ring_wait(step, slot):
        low = place((z + 8 - step) % 8, slot, 0, 64 if step == 4 else 128)
        arrived(low, up_recv.at[step - 1, slot], up_send.at[step - 1, slot])
        high_origin = (z + step) % 8
        high = place(high_origin, slot, 64, 64) if step == 4 else place(high_origin, slot)
        arrived(high, down_recv.at[step - 1, slot], down_send.at[step - 1, slot])

    ring_start(1, 0)
    to_pair = remote(
        own, place(z, 1), pair_send.at[0], pair_recv.at[0], at_dp(y2, z), me
    )
    to_pair.start()
    to_side = remote(
        weight_ref, weights.at[1], pair_send.at[1], pair_recv.at[1], at_dp(y1, z), me
    )

    to_other = remote(
        direct_ref, direct.at[1], pair_send.at[2], pair_recv.at[2], dp, tensor_of(x, 1 - h, c)
    )

    def ids_copy(i):
        to = (me + i) % 16
        return remote(
            ids_stage.at[i], ids_all.at[me], ids_send.at[i], ids_recv.at[me], dp, to
        )

    def ids_of(owner):
        slot = slots_ref[0, owner]
        value = ids_ref[0]
        for number in range(1, 4):
            value = jnp.where(slot >= 4 * number, ids_ref[number], value)
        return value

    ids_all[me] = ids_of(me)

    @pl.loop(1, 16)
    def _(i):
        ids_stage[i] = ids_of((me + i) % 16)
        ids_copy(i).start()

    first_row = (slots_ref[0, me] & 3) * 1024

    def count(low, high):
        @pl.loop(low, high)
        def _(i):
            source = (me + i) % 16

            @pl.when(i != 0)
            def _():
                arrived(ids_all.at[source], ids_recv.at[source], ids_send.at[i])

            ids = ids_all[source] - first_row
            digit = jnp.where((ids & 1) != 0, 16, 1) * jnp.where((ids & 2) != 0, 256, 1)
            digit = digit * jnp.where((ids & 4) != 0, 65536, 1)
            word = lax.shift_right_arithmetic(ids, 3)
            numbers = lax.broadcasted_iota(jnp.int32, (128, 256), 0)
            total = jnp.zeros((128, 256), jnp.int32)
            for bag in range(8):
                total = total + jnp.where(
                    numbers == word[bag : bag + 1, :], digit[bag : bag + 1, :], 0
                )
            packed[...] = total
            shifts = 4 * lax.broadcasted_iota(jnp.int32, (8, 256), 0)
            cols = pl.ds(pl.multiple_of((source // 4) * 256, 256), 256)

            @pl.loop(0, 8)
            def _(r):
                words = packed[pl.ds(pl.multiple_of(r * 16, 16), 16), :]
                for n in range(8):
                    both = [
                        lax.shift_right_logical(
                            jnp.broadcast_to(words[k : k + 1, :], (8, 256)), shifts
                        )
                        & 15
                        for k in (2 * n, 2 * n + 1)
                    ]
                    counts[
                        source % 4, pl.ds(pl.multiple_of(r * 128 + n * 16, 16), 16), cols
                    ] = jnp.concatenate(both).astype(F32).astype(BF16)

    m0 = z // 2
    pair_of = [m0, (m0 + 3 + 2 * odd) % 4, (m0 + 5 - 2 * odd) % 4, (m0 + 2) % 4]
    dest_x = (y + 2 * c) % 4
    ahead = (dest_x - x + 4) % 4

    def multiply(step, side):
        unit = 2 * step + side
        block = pair_of[step]

        @pl.loop(0, 2)
        def _(n):
            cols = pl.ds(pl.multiple_of(n * 256, 256), 256)
            part = jnp.dot(
                blocks[block], weights[side, :, cols], preferred_element_type=F32
            ).astype(BF16)
            partial[unit, 0, :, cols] = part[:256]
            partial[unit, 1, :, cols] = part[256:]

        remote(
            partial.at[unit, 1 - c], core_in.at[unit], core_send.at[unit], core_recv.at[unit],
            dp, tensor_of(x, h, 1 - c),
        ).start()

    def by_rows(body):
        @pl.loop(0, 4)
        def _(r):
            body(pl.ds(pl.multiple_of(r * 64, 64), 64))

    def send_on(step, side):
        unit = 2 * step + side
        to = tensor_of(dest_x, h, pair_of[step] % 2)

        @pl.when(ahead == 1)
        def _():
            remote(
                summed.at[0, unit], from_minus.at[unit], x_send.at[unit], minus_recv.at[unit], dp, to
            ).start()

        @pl.when(ahead == 3)
        def _():
            remote(
                summed.at[0, unit], from_plus.at[unit], x_send.at[unit], plus_recv.at[unit], dp, to
            ).start()

    def combine(step, side):
        unit = 2 * step + side
        arrived(core_in.at[unit], core_recv.at[unit], core_send.at[unit])

        def body(part):
            summed[0, unit, part, :] = (
                partial[unit, c, part, :].astype(F32) + core_in[unit, part, :].astype(F32)
            ).astype(BF16)

        by_rows(body)

        @pl.when((ahead == 0) & (c != pair_of[step] % 2))
        def _():
            remote(
                summed.at[0, unit], summed.at[1, unit], x_send.at[unit], own_recv.at[unit],
                dp, tensor_of(x, h, 1 - c),
            ).start()

        @pl.when(ahead == 2)
        def _():
            relay = (x + (1 if side == 0 else 3)) % 4
            remote(
                summed.at[0, unit], from_far.at[unit], x_send.at[unit], far_recv.at[unit],
                dp, tensor_of(relay, h, c),
            ).start()

        @pl.when(ahead == (3 if side == 0 else 1))
        def _():
            send_on(step, side)

    def relay_on(step, side):
        unit = 2 * step + side

        @pl.when(ahead == (1 if side == 0 else 3))
        def _():
            arrived(from_far.at[unit], far_recv.at[unit], x_send.at[unit])

            def body(part):
                summed[0, unit, part, :] = (
                    summed[0, unit, part, :].astype(F32) + from_far[unit, part, :].astype(F32)
                ).astype(BF16)

            by_rows(body)
            send_on(step, side)

    other_core = jnp.where((x == y) == (c == 0), 0, 1)

    def reduces(step):
        return active & (c == pair_of[step] % 2)

    def half_of(step):
        home = pair_of[step] // 2
        return (home - h) * (home - h)

    def final_remotes(step, side):
        unit = 2 * step + side
        half = half_of(step)
        same, across = 8 + 2 * half, 11 - 2 * half
        source = reduced.at[unit if side else same]
        copies = [
            remote(
                source, reduced.at[across], final_send.at[unit, 0], final_recv.at[across - 8],
                at_dp(y1 if side else y, z), tensor_of(x, 1 - h, c),
            )
        ]
        if side:
            copies.append(
                remote(
                    source, reduced.at[same], final_send.at[unit, 1], final_recv.at[same - 8],
                    at_dp(y1, z), me,
                )
            )
        return copies

    def reduce_x(step, side):
        unit = 2 * step + side

        @pl.when(reduces(step))
        def _():
            @pl.when(other_core == 1)
            def _():
                arrived(summed.at[1, unit], own_recv.at[unit], x_send.at[unit])

            arrived(from_minus.at[unit], minus_recv.at[unit], x_send.at[unit])
            arrived(from_plus.at[unit], plus_recv.at[unit], x_send.at[unit])
            target = unit if side else 8 + 2 * half_of(step)

            def body(part):
                reduced[target, part, :] = (
                    summed[other_core, unit, part, :].astype(F32)
                    + from_minus[unit, part, :].astype(F32)
                    + from_plus[unit, part, :].astype(F32)
                ).astype(BF16)

            by_rows(body)
            for copy in final_remotes(step, side):
                copy.start()

    def table_copy(half, i):
        spot = ((2 * x + c) + i) % 8
        to = tensor_of(spot // 2, h, spot % 2)
        source = tensor_of(x, (h + half) % 2, c)
        return remote(
            stage.at[half, i], table_grads.at[source % 4, source // 4], table_send.at[half, i],
            table_recv.at[source], dp, to,
        )

    def send_tables(half):
        source = tensor_of(x, (h + half) % 2, c)

        def chosen(owner):
            slot = slots_ref[0, owner]
            value = held[half, :, 0:128]
            for number in range(1, 4):
                columns = held[half, :, 128 * number : 128 * (number + 1)]
                value = jnp.where(slot >= 4 * number, columns, value)
            return value

        @pl.loop(1, 8)
        def _(i):
            spot = ((2 * x + c) + i) % 8
            stage[half, i] = chosen(tensor_of(spot // 2, h, spot % 2))
            table_copy(half, i).start()

        table_grads[source % 4, source // 4] = chosen(me)

    write_pooled = pltpu.make_async_copy(held.at[0], pooled_ref, local_sem.at[4])

    def finish(half):
        here, across = 8 + 2 * half, 9 + 2 * half

        @pl.when(jnp.logical_not(active))
        def _():
            arrived(reduced.at[here], final_recv.at[here - 8], final_send.at[0, 0])

        arrived(reduced.at[across], final_recv.at[across - 8], final_send.at[0, 0])

        def body(part):
            held[half, part, :] = (
                direct[half, part, :].astype(F32)
                + (reduced[here, part, :].astype(F32) + reduced[across, part, :].astype(F32))
            ).astype(BF16)

        by_rows(body)
        if half == 0:
            write_pooled.start()
        send_tables(half)

    def finish_step(step):
        @pl.when(c == pair_of[step] % 2)
        def _():
            @pl.when(half_of(step) == 0)
            def _():
                finish(0)

            @pl.when(half_of(step) == 1)
            def _():
                finish(1)

    def scatter(step):
        block = pair_of[step]

        @pl.loop(0, 4)
        def _(xx):
            source = 4 * xx + block

            @pl.when((xx != x) | (block % 2 != c))
            def _():
                arrived(table_grads.at[block, xx], table_recv.at[source], table_send.at[0, 1])

        part = jnp.dot(
            counts[block],
            table_grads[block].reshape(1024, 128),
            preferred_element_type=F32,
        )
        if step == 0:
            row_grad[...] = part
        else:
            row_grad[...] += part

    ring_wait(1, 0)
    ring_start(2, 0)
    to_side.start()
    count(0, 4)
    arrived(place(z, 1), pair_recv.at[0], pair_send.at[0])
    ring_start(1, 1)
    ring_wait(2, 0)
    ring_start(3, 0)
    count(4, 12)
    ring_wait(1, 1)
    ring_start(2, 1)
    loads[2].wait()
    multiply(0, 0)
    count(12, 16)
    ring_wait(3, 0)
    ring_start(4, 0)
    combine(0, 0)
    loads[3].wait()
    ring_wait(2, 1)
    ring_start(3, 1)
    multiply(1, 0)
    relay_on(0, 0)
    combine(1, 0)
    arrived(weights.at[1], pair_recv.at[1], pair_send.at[1])
    to_other.start()
    multiply(0, 1)
    multiply(1, 1)
    reduce_x(0, 0)
    combine(0, 1)
    combine(1, 1)
    relay_on(1, 0)
    ring_wait(3, 1)
    ring_start(4, 1)
    multiply(2, 0)
    multiply(2, 1)
    relay_on(0, 1)
    combine(2, 0)
    relay_on(1, 1)
    combine(2, 1)
    reduce_x(1, 0)
    ring_wait(4, 0)
    ring_wait(4, 1)
    multiply(3, 0)
    multiply(3, 1)
    combine(3, 0)
    combine(3, 1)
    reduce_x(0, 1)
    relay_on(2, 0)
    relay_on(2, 1)
    reduce_x(1, 1)
    relay_on(3, 0)
    reduce_x(2, 0)
    relay_on(3, 1)
    reduce_x(2, 1)
    reduce_x(3, 0)
    reduce_x(3, 1)
    arrived(direct.at[1], pair_recv.at[2], pair_send.at[2])
    finish_step(0)
    finish_step(1)
    finish_step(2)
    finish_step(3)
    scatter(0)
    scatter(1)
    scatter(2)
    scatter(3)
    write_rows = pltpu.make_async_copy(row_grad, row_grad_ref, local_sem.at[5])
    write_rows.start()

    for step in range(1, 5):
        for slot in range(2):
            ring_up(step, slot).wait_send()
            ring_down(step, slot).wait_send()
    to_pair.wait_send()
    to_side.wait_send()
    to_other.wait_send()

    @pl.loop(1, 16)
    def _(i):
        ids_copy(i).wait_send()

    for step in range(4):
        for side in range(2):
            unit = 2 * step + side
            sent(partial.at[unit, 0], core_send.at[unit], core_recv.at[unit])

            @pl.when((ahead != 0) | (c != pair_of[step] % 2))
            def _():
                sent(summed.at[0, unit], x_send.at[unit], own_recv.at[unit])

            @pl.when(reduces(step))
            def _():
                for copy in final_remotes(step, side):
                    copy.wait_send()

    @pl.loop(1, 8)
    def _(i):
        table_copy(0, i).wait_send()
        table_copy(1, i).wait_send()

    write_pooled.wait()
    write_rows.wait()


def local(
    emb_input, cross_grad, cross_weight, direct_grad, bag_ids, unit_slots, table_rows, adagrad_acc
):
    anywhere = pl.BlockSpec(memory_space=pl.ANY)
    dma = pltpu.SemaphoreType.DMA
    pooled, row_grad = pl.pallas_call(
        kernel,
        out_shape=(
            jax.ShapeDtypeStruct((256, 512), BF16),
            jax.ShapeDtypeStruct((1024, 128), F32),
        ),
        in_specs=[anywhere] * 4
        + [pl.BlockSpec(memory_space=pltpu.VMEM), pl.BlockSpec(memory_space=pltpu.SMEM)],
        out_specs=(anywhere,) * 2,
        scratch_shapes=[
            pltpu.VMEM((2, 128, 1024), BF16),
            pltpu.VMEM((4, 512, 1024), BF16),
            pltpu.VMEM((2, 1024, 512), BF16),
            pltpu.VMEM((2, 256, 512), BF16),
            pltpu.VMEM((8, 2, 256, 512), BF16),
            pltpu.VMEM((8, 256, 512), BF16),
            pltpu.VMEM((2, 8, 256, 512), BF16),
            pltpu.VMEM((8, 256, 512), BF16),
            pltpu.VMEM((8, 256, 512), BF16),
            pltpu.VMEM((8, 256, 512), BF16),
            pltpu.VMEM((12, 256, 512), BF16),
            pltpu.VMEM((2, 256, 512), BF16),
            pltpu.VMEM((2, 8, 256, 128), BF16),
            pltpu.VMEM((4, 4, 256, 128), BF16),
            pltpu.VMEM((16, 8, 256), jnp.int32),
            pltpu.VMEM((16, 8, 256), jnp.int32),
            pltpu.VMEM((128, 256), jnp.int32),
            pltpu.VMEM((4, 1024, 1024), BF16),
            pltpu.VMEM((1024, 128), F32),
            dma((6,)),
            dma((4, 2)),
            dma((4, 2)),
            dma((4, 2)),
            dma((4, 2)),
            dma((3,)),
            dma((3,)),
            dma((8,)),
            dma((8,)),
            dma((8,)),
            dma((8,)),
            dma((8,)),
            dma((8,)),
            dma((8,)),
            dma((8, 2)),
            dma((4,)),
            dma((2, 8)),
            dma((16,)),
            dma((16,)),
            dma((16,)),
        ],
        compiler_params=pltpu.CompilerParams(
            collective_id=1, has_side_effects=True, vmem_limit_bytes=56 * 2**20
        ),
        cost_estimate=pl.CostEstimate(
            flops=5_400_000_000, bytes_accessed=4_000_000, transcendentals=1024
        ),
    )(
        emb_input,
        cross_grad,
        cross_weight,
        direct_grad,
        jnp.transpose(bag_ids, (1, 2, 0)),
        unit_slots,
    )
    new_acc = adagrad_acc[0, 0] + jnp.mean(row_grad * row_grad, axis=-1)
    new_rows = table_rows[0, 0] - learn_rate * row_grad / jnp.sqrt(new_acc)[:, None]
    return (pooled, new_rows[None, None], new_acc[None, None])


def solution(mesh):
    return jax.shard_map(
        local,
        mesh=mesh,
        in_specs=(
            P("dp", "tensor"),
            P("dp", "tensor"),
            P("tensor", "dp"),
            P("tensor", "dp"),
            P("tensor", "dp", None),
            P("dp", None),
            P("dp", "tensor", None, None),
            P("dp", "tensor", None),
        ),
        out_specs=(P("tensor", "dp"), P("dp", "tensor", None, None), P("dp", "tensor", None)),
        check_vma=False,
    )
```

```python
import jax
import jax.numpy as jnp
from jax import lax
from jax.experimental import pallas as pl
from jax.experimental.pallas import tpu as pltpu
from jax.sharding import PartitionSpec as P

learn_rate = 0.5
F32 = jnp.float32
BF16 = jnp.bfloat16


def kernel(
    emb_ref, cross_ref, weight_ref, direct_ref, ids_ref, slots_ref,
    pooled_ref, row_grad_ref,
    factors, blocks, weights, direct,
    partial, core_in, summed, from_far, from_minus, from_plus, reduced,
    held, stage, table_grads, ids_stage, ids_all, packed, counts, row_grad,
    local_sem, up_send, up_recv, down_send, down_recv, pair_send, pair_recv,
    core_send, core_recv, x_send, far_recv, minus_recv, plus_recv, own_recv,
    final_send, final_recv, table_send, table_recv, ids_send, ids_recv,
):
    dp = lax.axis_index("dp")
    me = lax.axis_index("tensor")
    y, z = dp // 8, dp % 8
    x, h, c = me // 4, (me // 2) % 2, me % 2
    y1 = y + 1 - 2 * (y % 2)
    y2 = (y + 2) % 4
    active = x % 2 == y % 2
    odd = z % 2

    def tensor_of(xx, hh, cc):
        return (xx * 2 + hh) * 2 + cc

    def remote(src, dst, send, recv, to_dp, to_tensor):
        return pltpu.make_async_remote_copy(
            src_ref=src, dst_ref=dst, send_sem=send, recv_sem=recv,
            device_id=(to_dp, to_tensor), device_id_type=pl.DeviceIdType.MESH,
        )

    def arrived(dst, recv, send):
        remote(dst, dst, send, recv, dp, (me + 1) % 16).wait_recv()

    def sent(src, send, recv):
        remote(src, src, send, recv, dp, (me + 1) % 16).wait_send()

    def at_dp(yy, zz):
        return yy * 8 + zz

    barrier = pltpu.get_barrier_semaphore()

    def greet(to_dp, to_tensor):
        pl.semaphore_signal(
            barrier, inc=1, device_id=(to_dp, to_tensor), device_id_type=pl.DeviceIdType.MESH
        )

    up, down = (z + 1) % 8, (z + 7) % 8
    greet(at_dp(y, up), me)
    greet(at_dp(y, down), me)
    greet(at_dp(y2, z), me)
    greet(at_dp(y1, z), me)
    greet(at_dp(y1, z), tensor_of(x, 1 - h, c))

    @pl.loop(1, 16)
    def _(i):
        greet(dp, (me + i) % 16)

    loads = [
        pltpu.make_async_copy(emb_ref, factors.at[0], local_sem.at[0]),
        pltpu.make_async_copy(cross_ref, factors.at[1], local_sem.at[1]),
        pltpu.make_async_copy(weight_ref, weights.at[0], local_sem.at[2]),
        pltpu.make_async_copy(direct_ref, direct.at[0], local_sem.at[3]),
    ]
    for load in loads:
        load.start()
    loads[0].wait()
    loads[1].wait()

    def place(origin, slot, first=0, count=128):
        start = pl.multiple_of(slot * 256 + (origin % 2) * 128 + first, 64)
        return blocks.at[origin // 2, pl.ds(start, count), :]

    own = place(z, 0)
    own[...] = (factors[0].astype(F32) * factors[1].astype(F32)).astype(BF16)

    pl.semaphore_wait(barrier, 20)

    def ring_up(step, slot, part):
        ref = place((z + 9 - step) % 8, slot, 64 * part, 64)
        return remote(
            ref, ref, up_send.at[step - 1, slot, part], up_recv.at[step - 1, slot, part],
            at_dp(y, up), me,
        )

    def ring_down(step, slot, part):
        ref = place((z + step - 1) % 8, slot, 64 * part, 64)
        return remote(
            ref, ref, down_send.at[step - 1, slot, part], down_recv.at[step - 1, slot, part],
            at_dp(y, down), me,
        )

    def ring_copies(step, slot, part):
        copies = []
        if step < 4 or part == 0:
            copies.append(ring_up(step, slot, part))
        if step < 4 or part == 1:
            copies.append(ring_down(step, slot, part))
        return copies

    def ring_start(step, slot, parts=(0, 1)):
        for part in parts:
            for copy in ring_copies(step, slot, part):
                copy.start()

    def ring_wait(step, slot, parts=(0, 1)):
        for part in parts:
            if step < 4 or part == 0:
                arrived(
                    place((z + 8 - step) % 8, slot, 64 * part, 64),
                    up_recv.at[step - 1, slot, part], up_send.at[step - 1, slot, part],
                )
            if step < 4 or part == 1:
                arrived(
                    place((z + step) % 8, slot, 64 * part, 64),
                    down_recv.at[step - 1, slot, part], down_send.at[step - 1, slot, part],
                )

    def ring_pass(step, slot):
        for part in (0, 1):
            ring_wait(step, slot, (part,))
            ring_start(step + 1, slot, (part,))

    ring_start(1, 0)
    to_pair = [
        remote(
            place(z, 0, 64 * part, 64), place(z, 1, 64 * part, 64), pair_send.at[3 * part],
            pair_recv.at[3 * part], at_dp(y2, z), me,
        )
        for part in range(2)
    ]
    for copy in to_pair:
        copy.start()
    to_side = remote(
        weight_ref, weights.at[1], pair_send.at[1], pair_recv.at[1], at_dp(y1, z), me
    )

    to_other = remote(
        direct_ref, direct.at[1], pair_send.at[2], pair_recv.at[2], dp, tensor_of(x, 1 - h, c)
    )

    def ids_copy(i):
        to = (me + i) % 16
        return remote(
            ids_stage.at[i], ids_all.at[me], ids_send.at[i], ids_recv.at[me], dp, to
        )

    def ids_of(owner):
        slot = slots_ref[0, owner]
        value = ids_ref[0]
        for number in range(1, 4):
            value = jnp.where(slot >= 4 * number, ids_ref[number], value)
        return value

    ids_all[me] = ids_of(me)

    @pl.loop(1, 16)
    def _(i):
        ids_stage[i] = ids_of((me + i) % 16)
        ids_copy(i).start()

    first_row = (slots_ref[0, me] & 3) * 1024

    def count(low, high):
        @pl.loop(low, high)
        def _(i):
            source = (me + i) % 16

            @pl.when(i != 0)
            def _():
                arrived(ids_all.at[source], ids_recv.at[source], ids_send.at[i])

            ids = ids_all[source] - first_row
            digit = jnp.where((ids & 1) != 0, 16, 1) * jnp.where((ids & 2) != 0, 256, 1)
            digit = digit * jnp.where((ids & 4) != 0, 65536, 1)
            word = lax.shift_right_arithmetic(ids, 3)
            numbers = lax.broadcasted_iota(jnp.int32, (128, 256), 0)
            total = jnp.zeros((128, 256), jnp.int32)
            for bag in range(8):
                total = total + jnp.where(
                    numbers == word[bag : bag + 1, :], digit[bag : bag + 1, :], 0
                )
            packed[...] = total
            shifts = 4 * lax.broadcasted_iota(jnp.int32, (8, 256), 0)
            cols = pl.ds(pl.multiple_of((source // 4) * 256, 256), 256)

            @pl.loop(0, 8)
            def _(r):
                words = packed[pl.ds(pl.multiple_of(r * 16, 16), 16), :]
                for n in range(8):
                    both = [
                        lax.shift_right_logical(
                            jnp.broadcast_to(words[k : k + 1, :], (8, 256)), shifts
                        )
                        & 15
                        for k in (2 * n, 2 * n + 1)
                    ]
                    counts[
                        source % 4, pl.ds(pl.multiple_of(r * 128 + n * 16, 16), 16), cols
                    ] = jnp.concatenate(both).astype(F32).astype(BF16)

    m0 = z // 2
    pair_of = [m0, (m0 + 3 + 2 * odd) % 4, (m0 + 5 - 2 * odd) % 4, (m0 + 2) % 4]
    dest_x = (y + 2 * c) % 4
    ahead = (dest_x - x + 4) % 4

    def multiply(step, side):
        unit = 2 * step + side
        block = pair_of[step]

        @pl.loop(0, 2)
        def _(n):
            cols = pl.ds(pl.multiple_of(n * 256, 256), 256)
            part = jnp.dot(
                blocks[block], weights[side, :, cols], preferred_element_type=F32
            ).astype(BF16)
            partial[unit, 0, :, cols] = part[:256]
            partial[unit, 1, :, cols] = part[256:]

        remote(
            partial.at[unit, 1 - c], core_in.at[unit], core_send.at[unit], core_recv.at[unit],
            dp, tensor_of(x, h, 1 - c),
        ).start()

    def by_rows(body):
        @pl.loop(0, 4)
        def _(r):
            body(pl.ds(pl.multiple_of(r * 64, 64), 64))

    def send_on(step, side):
        unit = 2 * step + side
        to = tensor_of(dest_x, h, pair_of[step] % 2)

        @pl.when(ahead == 1)
        def _():
            remote(
                summed.at[0, unit], from_minus.at[unit], x_send.at[unit], minus_recv.at[unit], dp, to
            ).start()

        @pl.when(ahead == 3)
        def _():
            remote(
                summed.at[0, unit], from_plus.at[unit], x_send.at[unit], plus_recv.at[unit], dp, to
            ).start()

    def combine(step, side):
        unit = 2 * step + side
        arrived(core_in.at[unit], core_recv.at[unit], core_send.at[unit])

        def body(part):
            summed[0, unit, part, :] = (
                partial[unit, c, part, :].astype(F32) + core_in[unit, part, :].astype(F32)
            ).astype(BF16)

        by_rows(body)

        @pl.when((ahead == 0) & (c != pair_of[step] % 2))
        def _():
            remote(
                summed.at[0, unit], summed.at[1, unit], x_send.at[unit], own_recv.at[unit],
                dp, tensor_of(x, h, 1 - c),
            ).start()

        @pl.when(ahead == 2)
        def _():
            relay = (x + (1 if side == 0 else 3)) % 4
            remote(
                summed.at[0, unit], from_far.at[unit], x_send.at[unit], far_recv.at[unit],
                dp, tensor_of(relay, h, c),
            ).start()

        @pl.when(ahead == (3 if side == 0 else 1))
        def _():
            send_on(step, side)

    def relay_on(step, side):
        unit = 2 * step + side

        @pl.when(ahead == (1 if side == 0 else 3))
        def _():
            arrived(from_far.at[unit], far_recv.at[unit], x_send.at[unit])

            def body(part):
                summed[0, unit, part, :] = (
                    summed[0, unit, part, :].astype(F32) + from_far[unit, part, :].astype(F32)
                ).astype(BF16)

            by_rows(body)
            send_on(step, side)

    other_core = jnp.where((x == y) == (c == 0), 0, 1)

    def reduces(step):
        return active & (c == pair_of[step] % 2)

    def half_of(step):
        home = pair_of[step] // 2
        return (home - h) * (home - h)

    def final_remotes(step, side):
        unit = 2 * step + side
        half = half_of(step)
        same, across = 8 + 2 * half, 11 - 2 * half
        source = reduced.at[unit if side else same]
        copies = [
            remote(
                source, reduced.at[across], final_send.at[unit, 0], final_recv.at[across - 8],
                at_dp(y1 if side else y, z), tensor_of(x, 1 - h, c),
            )
        ]
        if side:
            copies.append(
                remote(
                    source, reduced.at[same], final_send.at[unit, 1], final_recv.at[same - 8],
                    at_dp(y1, z), me,
                )
            )
        return copies

    def reduce_x(step, side):
        unit = 2 * step + side

        @pl.when(reduces(step))
        def _():
            @pl.when(other_core == 1)
            def _():
                arrived(summed.at[1, unit], own_recv.at[unit], x_send.at[unit])

            arrived(from_minus.at[unit], minus_recv.at[unit], x_send.at[unit])
            arrived(from_plus.at[unit], plus_recv.at[unit], x_send.at[unit])
            target = unit if side else 8 + 2 * half_of(step)

            def body(part):
                reduced[target, part, :] = (
                    summed[other_core, unit, part, :].astype(F32)
                    + from_minus[unit, part, :].astype(F32)
                    + from_plus[unit, part, :].astype(F32)
                ).astype(BF16)

            by_rows(body)
            for copy in final_remotes(step, side):
                copy.start()

    def table_copy(half, i):
        spot = ((2 * x + c) + i) % 8
        to = tensor_of(spot // 2, h, spot % 2)
        source = tensor_of(x, (h + half) % 2, c)
        return remote(
            stage.at[half, i], table_grads.at[source % 4, source // 4], table_send.at[half, i],
            table_recv.at[source], dp, to,
        )

    def send_tables(half):
        source = tensor_of(x, (h + half) % 2, c)

        def chosen(owner):
            slot = slots_ref[0, owner]
            value = held[half, :, 0:128]
            for number in range(1, 4):
                columns = held[half, :, 128 * number : 128 * (number + 1)]
                value = jnp.where(slot >= 4 * number, columns, value)
            return value

        @pl.loop(1, 8)
        def _(i):
            spot = ((2 * x + c) + i) % 8
            stage[half, i] = chosen(tensor_of(spot // 2, h, spot % 2))
            table_copy(half, i).start()

        table_grads[source % 4, source // 4] = chosen(me)

    write_pooled = pltpu.make_async_copy(held.at[0], pooled_ref, local_sem.at[4])

    def finish(half):
        here, across = 8 + 2 * half, 9 + 2 * half

        @pl.when(jnp.logical_not(active))
        def _():
            arrived(reduced.at[here], final_recv.at[here - 8], final_send.at[0, 0])

        arrived(reduced.at[across], final_recv.at[across - 8], final_send.at[0, 0])

        def body(part):
            held[half, part, :] = (
                direct[half, part, :].astype(F32)
                + (reduced[here, part, :].astype(F32) + reduced[across, part, :].astype(F32))
            ).astype(BF16)

        by_rows(body)
        if half == 0:
            write_pooled.start()
        send_tables(half)

    def finish_step(step):
        @pl.when(c == pair_of[step] % 2)
        def _():
            @pl.when(half_of(step) == 0)
            def _():
                finish(0)

            @pl.when(half_of(step) == 1)
            def _():
                finish(1)

    def scatter(step):
        block = pair_of[step]

        @pl.loop(0, 4)
        def _(xx):
            source = 4 * xx + block

            @pl.when((xx != x) | (block % 2 != c))
            def _():
                arrived(table_grads.at[block, xx], table_recv.at[source], table_send.at[0, 1])

        part = jnp.dot(
            counts[block],
            table_grads[block].reshape(1024, 128),
            preferred_element_type=F32,
        )
        if step == 0:
            row_grad[...] = part
        else:
            row_grad[...] += part

    to_side.start()
    ring_pass(1, 0)
    count(0, 4)
    for part in range(2):
        arrived(place(z, 1, 64 * part, 64), pair_recv.at[3 * part], pair_send.at[3 * part])
        ring_start(1, 1, (part,))
    ring_pass(2, 0)
    count(4, 12)
    ring_pass(1, 1)
    loads[2].wait()
    multiply(0, 0)
    count(12, 16)
    ring_pass(3, 0)
    combine(0, 0)
    loads[3].wait()
    ring_pass(2, 1)
    multiply(1, 0)
    relay_on(0, 0)
    combine(1, 0)
    arrived(weights.at[1], pair_recv.at[1], pair_send.at[1])
    to_other.start()
    multiply(0, 1)
    multiply(1, 1)
    reduce_x(0, 0)
    combine(0, 1)
    combine(1, 1)
    relay_on(1, 0)
    ring_pass(3, 1)
    multiply(2, 0)
    multiply(2, 1)
    relay_on(0, 1)
    combine(2, 0)
    relay_on(1, 1)
    combine(2, 1)
    reduce_x(1, 0)
    ring_wait(4, 0)
    ring_wait(4, 1)
    multiply(3, 0)
    multiply(3, 1)
    relay_on(2, 0)
    combine(3, 0)
    relay_on(2, 1)
    combine(3, 1)
    reduce_x(0, 1)
    reduce_x(1, 1)
    relay_on(3, 0)
    reduce_x(2, 0)
    relay_on(3, 1)
    reduce_x(2, 1)
    arrived(direct.at[1], pair_recv.at[2], pair_send.at[2])
    finish_step(0)
    finish_step(1)
    reduce_x(3, 0)
    reduce_x(3, 1)
    scatter(0)
    finish_step(2)
    finish_step(3)
    scatter(1)
    scatter(2)
    scatter(3)
    write_rows = pltpu.make_async_copy(row_grad, row_grad_ref, local_sem.at[5])
    write_rows.start()

    for step in range(1, 5):
        for slot in range(2):
            for part in range(2):
                for copy in ring_copies(step, slot, part):
                    copy.wait_send()
    for copy in to_pair:
        copy.wait_send()
    to_side.wait_send()
    to_other.wait_send()

    @pl.loop(1, 16)
    def _(i):
        ids_copy(i).wait_send()

    for step in range(4):
        for side in range(2):
            unit = 2 * step + side
            sent(partial.at[unit, 0], core_send.at[unit], core_recv.at[unit])

            @pl.when((ahead != 0) | (c != pair_of[step] % 2))
            def _():
                sent(summed.at[0, unit], x_send.at[unit], own_recv.at[unit])

            @pl.when(reduces(step))
            def _():
                for copy in final_remotes(step, side):
                    copy.wait_send()

    @pl.loop(1, 8)
    def _(i):
        table_copy(0, i).wait_send()
        table_copy(1, i).wait_send()

    write_pooled.wait()
    write_rows.wait()


def local(
    emb_input, cross_grad, cross_weight, direct_grad, bag_ids, unit_slots, table_rows, adagrad_acc
):
    anywhere = pl.BlockSpec(memory_space=pl.ANY)
    dma = pltpu.SemaphoreType.DMA
    pooled, row_grad = pl.pallas_call(
        kernel,
        out_shape=(
            jax.ShapeDtypeStruct((256, 512), BF16),
            jax.ShapeDtypeStruct((1024, 128), F32),
        ),
        in_specs=[anywhere] * 4
        + [pl.BlockSpec(memory_space=pltpu.VMEM), pl.BlockSpec(memory_space=pltpu.SMEM)],
        out_specs=(anywhere,) * 2,
        scratch_shapes=[
            pltpu.VMEM((2, 128, 1024), BF16),
            pltpu.VMEM((4, 512, 1024), BF16),
            pltpu.VMEM((2, 1024, 512), BF16),
            pltpu.VMEM((2, 256, 512), BF16),
            pltpu.VMEM((8, 2, 256, 512), BF16),
            pltpu.VMEM((8, 256, 512), BF16),
            pltpu.VMEM((2, 8, 256, 512), BF16),
            pltpu.VMEM((8, 256, 512), BF16),
            pltpu.VMEM((8, 256, 512), BF16),
            pltpu.VMEM((8, 256, 512), BF16),
            pltpu.VMEM((12, 256, 512), BF16),
            pltpu.VMEM((2, 256, 512), BF16),
            pltpu.VMEM((2, 8, 256, 128), BF16),
            pltpu.VMEM((4, 4, 256, 128), BF16),
            pltpu.VMEM((16, 8, 256), jnp.int32),
            pltpu.VMEM((16, 8, 256), jnp.int32),
            pltpu.VMEM((128, 256), jnp.int32),
            pltpu.VMEM((4, 1024, 1024), BF16),
            pltpu.VMEM((1024, 128), F32),
            dma((6,)),
            dma((4, 2, 2)),
            dma((4, 2, 2)),
            dma((4, 2, 2)),
            dma((4, 2, 2)),
            dma((4,)),
            dma((4,)),
            dma((8,)),
            dma((8,)),
            dma((8,)),
            dma((8,)),
            dma((8,)),
            dma((8,)),
            dma((8,)),
            dma((8, 2)),
            dma((4,)),
            dma((2, 8)),
            dma((16,)),
            dma((16,)),
            dma((16,)),
        ],
        compiler_params=pltpu.CompilerParams(
            collective_id=1, has_side_effects=True, vmem_limit_bytes=56 * 2**20
        ),
        cost_estimate=pl.CostEstimate(
            flops=5_400_000_000, bytes_accessed=4_000_000, transcendentals=1024
        ),
    )(
        emb_input,
        cross_grad,
        cross_weight,
        direct_grad,
        jnp.transpose(bag_ids, (1, 2, 0)),
        unit_slots,
    )
    new_acc = adagrad_acc[0, 0] + jnp.mean(row_grad * row_grad, axis=-1)
    new_rows = table_rows[0, 0] - learn_rate * row_grad / jnp.sqrt(new_acc)[:, None]
    return (pooled, new_rows[None, None], new_acc[None, None])


def solution(mesh):
    return jax.shard_map(
        local,
        mesh=mesh,
        in_specs=(
            P("dp", "tensor"),
            P("dp", "tensor"),
            P("tensor", "dp"),
            P("tensor", "dp"),
            P("tensor", "dp", None),
            P("dp", None),
            P("dp", "tensor", None, None),
            P("dp", "tensor", None),
        ),
        out_specs=(P("tensor", "dp"), P("dp", "tensor", None, None), P("dp", "tensor", None)),
        check_vma=False,
    )
```
